32 devices in a mesh: groups: 2 (over y), ctx: 8 (over z, x), tp: 2 (over core).
Axes of the slice: x: 2, y: 2, z: 4, core: 2. Of those that a mesh axis runs over, the one named last changes fastest.
Arguments:
- normed_input: bfloat16 [4096, 2688], P(('groups', 'ctx')), parts along dimension 0, may hold values from -6 to 6
- attn_queries: bfloat16 [4096, 2048], P(('groups', 'ctx'), 'tp'), parts along dimension 0, may hold values from -45 to 45
- attn_keys: bfloat16 [4096, 1024], P(('groups', 'ctx'), 'tp'), parts along dimension 0, may hold values from -9 to 9
- attn_values: bfloat16 [4096, 1024], P(('groups', 'ctx'), 'tp'), parts along dimension 0, may hold values from -6 to 6
- out_grad: bfloat16 [4096, 2048], P(('groups', 'ctx'), 'tp'), parts along dimension 0, may hold values from -6 to 6
Outputs:
- query_grad: bfloat16 [4096, 2048], P(('groups', 'ctx'), 'tp'), parts along dimension 0
- key_weight_grad: float32 [5376, 1024], P(('groups', 'ctx'), 'tp'), parts along dimension 0
- value_grad: bfloat16 [4096, 1024], P(('groups', 'ctx'), 'tp'), parts along dimension 0
The draws below stay inside these ranges and needn't reach their ends.
There are 2 independent parts, one for each index of `groups`. The reference program is written for one: setup_inputs(seed, part) draws one part's arguments, and reference() takes and returns one part's arrays. A program takes and returns all parts, laid end to end along the dimension named above; each array names one. Nothing has to cross between parts.
All inputs are finite; a program needn't handle non-finite values.
Results may differ from the reference program's by a relative error of at most 0.0053.
Values may be sent and summed in bfloat16 or wider, within the bound.
A program may use at most 128 MiB of HBM per device.

```python
import jax
import jax.numpy as jnp
from jax import lax

D = 2688
HD = 128
HQ = 16
HK = 8
W = 1024
TOKENS = 2048


def paired_draw(base_key):
    query_seed = jax.random.fold_in(base_key, 101)
    keys_seed = jax.random.fold_in(base_key, 202)
    key_part = jax.random.truncated_normal(keys_seed, -4.0, 4.0, (TOKENS, HK * HD), jnp.float32)
    query_part = jax.random.truncated_normal(query_seed, -4.0, 4.0, (TOKENS, HQ * HD), jnp.float32)
    return (query_part, key_part)


def draw_attn_queries(key, part):
    return paired_draw(key)[0].astype(jnp.bfloat16)


def draw_attn_keys(key, part):
    return paired_draw(key)[1].astype(jnp.bfloat16)


def with_spikes(array, key, source, target, blocks, factor):
    def block_of(axis_at):
        return (jnp.arange(array.shape[axis_at]) // (array.shape[axis_at] // blocks)).reshape((-1,) + (1,) * (array.ndim - 1 - axis_at))

    near = jax.random.permutation(key, blocks)[block_of(target)]
    other_side = (block_of(target) + blocks // 2) % blocks
    return jnp.where((block_of(source) == near) | (block_of(source) == other_side), factor * array, array)


def levels(stream_key, shape, split, least, high):
    loudness, own = 1.0, jax.random.fold_in(stream_key, 6)
    for position, blocks in split:
        draws = jnp.exp(jax.random.uniform(jax.random.fold_in(own, position), (blocks,), jnp.float32, least / len(split), high / len(split)))
        loudness = loudness * jnp.repeat(draws, shape[position] // blocks).reshape([-1 if axis == position else 1 for axis in range(len(shape))])
    return loudness


def noise(own_key, extent, deviation, reach, split=(), kind=jnp.bfloat16):
    values = deviation * jax.random.normal(own_key, extent, jnp.float32)
    if split:
        values = values * levels(own_key, extent, split, -0.22, 0.18)
    return jnp.clip(values, -reach, reach).astype(kind)


def noise_with(key, dims, width, limit, split, heavy, kind=jnp.bfloat16):
    array = width * jax.random.normal(key, dims, jnp.float32)
    if split:
        array = array * levels(key, dims, split, -0.22, 0.18)
    return jnp.clip(with_spikes(array, jax.random.fold_in(key, 3), *heavy), -limit, limit).astype(kind)


def setup_inputs(seed: int = 0, part: int = 0) -> dict:
    arg_keys = jax.random.split(jax.random.key(seed), 6)
    part_splits = jax.random.split(jax.random.fold_in(arg_keys[5], part), 6)
    return {
        "normed_input": noise_with(part_splits[0], (TOKENS, D), 1.0, 6.0, ((0, 8),), (0, 1, 8, 2.0)),
        "attn_queries": draw_attn_queries(jax.random.fold_in(jax.random.fold_in(arg_keys[5], part), 71), part),
        "attn_keys": draw_attn_keys(jax.random.fold_in(jax.random.fold_in(arg_keys[5], part), 71), part),
        "attn_values": noise(part_splits[3], (TOKENS, HK * HD), 1.0, 6.0, ((0, 8), (1, 2))),
        "out_grad": noise(part_splits[4], (TOKENS, HQ * HD), 1.0, 6.0, ((0, 8), (1, 2))),
    }


attn_scale = 168.0 ** -0.5


def reference(normed_input, attn_queries, attn_keys, attn_values, out_grad):
    group_size = HQ // HK
    block_rows = min(512, TOKENS)
    window_rows = block_rows + W
    kv_width = HK * HD
    pad_keys = jnp.concatenate([jnp.zeros((W, kv_width), jnp.bfloat16), attn_keys], axis=0)
    pad_values = jnp.concatenate([jnp.zeros((W, kv_width), jnp.bfloat16), attn_values], axis=0)
    query_offsets = jnp.arange(block_rows, dtype=jnp.int32)
    key_offsets = jnp.arange(window_rows, dtype=jnp.int32)

    def one_block(carry, block_index):
        key_total, value_total = carry
        row_start = (block_index * block_rows).astype(jnp.int32)
        query_block = lax.dynamic_slice_in_dim(attn_queries, row_start, block_rows, 0).astype(jnp.float32).reshape(block_rows, HK, group_size, HD)
        grad_block = lax.dynamic_slice_in_dim(out_grad, row_start, block_rows, 0).astype(jnp.float32).reshape(block_rows, HK, group_size, HD)
        key_block = lax.dynamic_slice_in_dim(pad_keys, row_start, window_rows, 0).astype(jnp.float32).reshape(window_rows, HK, HD)
        value_block = lax.dynamic_slice_in_dim(pad_values, row_start, window_rows, 0).astype(jnp.float32).reshape(window_rows, HK, HD)
        query_pos = row_start + query_offsets
        key_pos = row_start - W + key_offsets
        distance_back = query_pos[:, None] - key_pos[None, :]
        allowed = (distance_back >= 0) & (distance_back < W) & (key_pos[None, :] >= 0)
        scores = attn_scale * jnp.einsum("qhgd,khd->hgqk", query_block, key_block)
        scores = jnp.where(allowed, scores, -jnp.inf)
        row_max = jnp.max(scores, axis=-1, keepdims=True)
        raised = jnp.exp(scores - row_max)
        soft_weights = raised / jnp.sum(raised, axis=-1, keepdims=True)
        soft_low = lax.optimization_barrier(soft_weights.astype(jnp.bfloat16)).astype(jnp.float32)
        grad_probs = jnp.einsum("qhgd,khd->hgqk", grad_block, value_block)
        row_delta = jnp.sum(soft_weights * grad_probs, axis=-1, keepdims=True)
        grad_scores = lax.optimization_barrier((soft_weights * (grad_probs - row_delta)).astype(jnp.bfloat16)).astype(jnp.float32)
        grad_query = (attn_scale * jnp.einsum("hgqk,khd->qhgd", grad_scores, key_block)).astype(jnp.bfloat16).reshape(block_rows, HQ * HD)
        key_part = (attn_scale * jnp.einsum("hgqk,qhgd->khd", grad_scores, query_block)).reshape(window_rows, kv_width)
        value_part = jnp.einsum("hgqk,qhgd->khd", soft_low, grad_block).reshape(window_rows, kv_width)
        key_total = lax.dynamic_update_slice_in_dim(key_total, lax.dynamic_slice_in_dim(key_total, row_start, window_rows, 0) + key_part, row_start, 0)
        value_total = lax.dynamic_update_slice_in_dim(value_total, lax.dynamic_slice_in_dim(value_total, row_start, window_rows, 0) + value_part, row_start, 0)
        return (key_total, value_total), grad_query

    zero_rows = jnp.zeros((TOKENS + W, kv_width), jnp.float32)
    (key_total, value_total), grad_rows = lax.scan(one_block, (zero_rows, zero_rows), jnp.arange(TOKENS // block_rows, dtype=jnp.int32))
    query_grad = grad_rows.reshape(TOKENS, HQ * HD)
    key_low = key_total[W:].astype(jnp.bfloat16)
    value_low = value_total[W:].astype(jnp.bfloat16)
    key_weight_grad = jnp.dot(normed_input.T, key_low, preferred_element_type=jnp.float32)
    return (query_grad, key_weight_grad, value_low)
```

```python
import functools

import jax
import jax.numpy as jnp
from jax import lax
from jax.experimental import pallas as pl
from jax.experimental.pallas import tpu as pltpu
from jax.sharding import PartitionSpec as P

HD = 128
GROUP = 2
W = 1024
REACH = 4

attn_scale = 168.0 ** (-0.5)
LOG2E = 1.4426950408889634
NEG = -1e30
MESH = pl.DeviceIdType.MESH
F32 = jnp.float32
BF16 = jnp.bfloat16


def dot_nt(a, b):
    return lax.dot_general(a, b, (((1,), (1,)), ((), ())), preferred_element_type=F32)


def dot_nn(a, b):
    return lax.dot_general(a, b, (((1,), (0,)), ((), ())), preferred_element_type=F32)


def dot_tn(a, b):
    return lax.dot_general(a, b, (((0,), (0,)), ((), ())), preferred_element_type=F32)


def attention(
    n,
    nh,
    rows,
    q_ref,
    k_ref,
    v_ref,
    g_ref,
    dq_ref,
    dk_ref,
    dv_ref,
    buf,
    qp,
    gp,
    acc,
    sb,
    rv,
    s_sc,
    send_f,
    recv_f,
    send_r,
    recv_r,
):
    c = lax.axis_index("ctx")
    x = lax.rem(c, 2)
    even = x == 0
    odd = x == 1
    pair = c + 1 - 2 * x
    up = c + 2 < n
    down = c >= 2

    barrier = pltpu.get_barrier_semaphore()

    def greet(target):
        pl.semaphore_signal(barrier, inc=1, device_id={"ctx": target}, device_id_type=MESH)

    greet(pair)
    pl.when(up)(lambda: greet(c + 2))
    pl.when(down)(lambda: greet(c - 2))

    def cols(h, width):
        return pl.ds(pl.multiple_of(h * width, width), width)

    def pack(h, carry):
        buf[0, h, 0] = k_ref[:, cols(h, HD)]
        buf[0, h, 1] = v_ref[:, cols(h, HD)]
        return carry

    lax.fori_loop(0, nh, pack, 0)

    pl.semaphore_wait(barrier, 1 + up.astype(jnp.int32) + down.astype(jnp.int32))

    def halo(src, dst, h, target):
        return pltpu.make_async_remote_copy(
            src_ref=buf.at[src, h],
            dst_ref=buf.at[dst, h],
            send_sem=send_f.at[dst - 1, h],
            recv_sem=recv_f.at[dst - 1, h],
            device_id={"ctx": target},
            device_id_type=MESH,
        )

    def back(d, h, target):
        return pltpu.make_async_remote_copy(
            src_ref=sb.at[d - 1, h],
            dst_ref=rv.at[d - 1, h],
            send_sem=send_r.at[d - 1, h],
            recv_sem=recv_r.at[d - 1, h],
            device_id={"ctx": target},
            device_id_type=MESH,
        )

    def send_own(h):
        pl.when(up)(lambda: halo(0, 2, h, c + 2).start())
        pl.when(even)(lambda: halo(0, 1, h, c + 1).start())

    send_own(0)
    send_own(1)

    def pack_q(h, carry):
        for i in range(GROUP):
            qp[h, i * rows : (i + 1) * rows] = q_ref[:, cols(h * GROUP + i, HD)]
            gp[h, i * rows : (i + 1) * rows] = g_ref[:, cols(h * GROUP + i, HD)]
        return carry

    lax.fori_loop(0, nh, pack_q, 0)

    for d in range(1, REACH + 1):

        @pl.when(c < d)
        def _():
            buf[d] = jnp.zeros(buf.shape[1:], BF16)

    def forward(h):
        @pl.when(down)
        def _():
            halo(0, 2, h, pair).wait_recv()

            @pl.when(up)
            def _():
                halo(2, 4, h, c + 2).start()

            @pl.when(even)
            def _():
                halo(2, 3, h, pair).start()

            @pl.when(odd)
            def _():
                halo(2, 1, h, pair).start()

        @pl.when(h + 2 < nh)
        def _():
            send_own(h + 2)

        @pl.when(c >= 4)
        def _():
            halo(2, 4, h, pair).wait_recv()

            @pl.when(odd)
            def _():
                halo(4, 3, h, pair).start()

        pl.when(c >= 1)(lambda: halo(0, 1, h, pair).wait_recv())
        pl.when(c >= 3)(lambda: halo(0, 3, h, pair).wait_recv())

    wide = GROUP * rows
    key_at = lax.broadcasted_iota(jnp.int32, (rows, wide), 0)
    query_at = lax.rem(lax.broadcasted_iota(jnp.int32, (rows, wide), 1), rows)

    def compute(h):
        q = qp[h]
        g = gp[h]
        tri = key_at <= query_at
        factor = attn_scale * LOG2E
        far = jnp.where(c >= 4, 0.0, NEG)
        s0 = jnp.where(tri, dot_nt(buf[0, h, 0], q) * factor, dot_nt(buf[4, h, 0], q) * factor + far)
        s_sc[0] = s0
        top = jnp.max(s0, axis=0, keepdims=True)
        for d in range(1, REACH):
            s = dot_nt(buf[d, h, 0], q) * factor + jnp.where(c >= d, 0.0, NEG)
            s_sc[d] = s
            top = jnp.maximum(top, jnp.max(s, axis=0, keepdims=True))
        total = jnp.zeros((1, wide), F32)
        delta = jnp.zeros((1, wide), F32)
        for d in range(REACH):
            e = jnp.exp2(s_sc[d] - top)
            if d == 0:
                gpr = jnp.where(tri, dot_nt(buf[0, h, 1], g), dot_nt(buf[4, h, 1], g))
            else:
                gpr = dot_nt(buf[d, h, 1], g)
            total += jnp.sum(e, axis=0, keepdims=True)
            delta += jnp.sum(e * gpr, axis=0, keepdims=True)
            s_sc[d] = e
            s_sc[REACH + d] = gpr
        inv = 1.0 / total
        delta = delta * inv
        dq = jnp.zeros((HD, wide), F32)
        for d in range(REACH):
            p = s_sc[d] * inv
            ds = p * (s_sc[REACH + d] - delta)
            if d == 0:
                parts = (
                    (0, jnp.where(tri, p, 0.0), jnp.where(tri, ds, 0.0)),
                    (4, jnp.where(tri, 0.0, p), jnp.where(tri, 0.0, ds)),
                )
            else:
                parts = ((d, p, ds),)
            for slot, p_part, ds_part in parts:
                p_low = p_part.astype(BF16)
                ds_low = ds_part.astype(BF16)
                dk = attn_scale * dot_nn(ds_low, q)
                dv = dot_nn(p_low, g)
                dq += dot_tn(buf[slot, h, 0], ds_low)
                if slot % 2:
                    sb[slot - 1, h, 0] = dk.astype(BF16)
                    sb[slot - 1, h, 1] = dv.astype(BF16)
                else:
                    acc[slot // 2, h, 0] = dk
                    acc[slot // 2, h, 1] = dv
        dq = (dq * attn_scale).T.astype(BF16)
        for i in range(GROUP):
            dq_ref[:, cols(h * GROUP + i, HD)] = dq[i * rows : (i + 1) * rows]

        pl.when(c >= 1)(lambda: back(1, h, pair).start())
        pl.when(c >= 3)(lambda: back(3, h, pair).start())

    def add(slot, d, h):
        acc[slot, h] += rv[d - 1, h].astype(F32)

    def stage_b(h):
        @pl.when(pair >= 3)
        def _():
            back(3, h, pair).wait_recv()
            pl.when(odd)(lambda: add(2, 3, h))
            pl.when(even)(lambda: add(1, 3, h))

        @pl.when(c >= 4)
        def _():
            sb[3, h] = acc[2, h].astype(BF16)
            back(4, h, c - 2).start()

        @pl.when(pair >= 1)
        def _():
            back(1, h, pair).wait_recv()
            pl.when(odd)(lambda: add(1, 1, h))
            pl.when(even)(lambda: add(0, 1, h))

    def stage_c(h):
        @pl.when(down)
        def _():
            @pl.when(up)
            def _():
                back(4, h, pair).wait_recv()
                add(1, 4, h)

            sb[1, h] = acc[1, h].astype(BF16)
            back(2, h, c - 2).start()

    def stage_d(h):
        @pl.when(up)
        def _():
            back(2, h, pair).wait_recv()
            add(0, 2, h)

        dk_ref[:, cols(h, HD)] = acc[0, h, 0].astype(BF16)
        dv_ref[:, cols(h, HD)] = acc[0, h, 1].astype(BF16)

    def step(i, carry):
        @pl.when(i < nh)
        def _():
            forward(i)
            compute(i)

        @pl.when((i >= 1) & (i < nh + 1))
        def _():
            stage_b(i - 1)

        @pl.when((i >= 2) & (i < nh + 2))
        def _():
            stage_c(i - 2)

        @pl.when(i >= 3)
        def _():
            stage_d(i - 3)

        return carry

    lax.fori_loop(0, nh + 3, step, 0)

    def drain(h, carry):
        pl.when(up)(lambda: halo(0, 2, h, pair).wait_send())
        pl.when(even)(lambda: halo(0, 1, h, pair).wait_send())
        pl.when(down & up)(lambda: halo(2, 4, h, pair).wait_send())
        pl.when(down & even)(lambda: halo(2, 3, h, pair).wait_send())
        pl.when(down & odd)(lambda: halo(2, 1, h, pair).wait_send())
        pl.when((c >= 4) & odd)(lambda: halo(4, 3, h, pair).wait_send())
        pl.when(c >= 1)(lambda: back(1, h, pair).wait_send())
        pl.when(c >= 3)(lambda: back(3, h, pair).wait_send())
        pl.when(c >= 4)(lambda: back(4, h, pair).wait_send())
        pl.when(down)(lambda: back(2, h, pair).wait_send())
        return carry

    lax.fori_loop(0, nh, drain, 0)


def shards(n, normed_input, attn_queries, attn_keys, attn_values, out_grad):
    rows = attn_queries.shape[0]
    nh = attn_keys.shape[1] // HD
    assert rows * REACH == W and n % 2 == 0
    block = (2, rows, HD)
    vmem = pl.BlockSpec(memory_space=pltpu.VMEM)
    query_grad, key_low, value_low = pl.pallas_call(
        functools.partial(attention, n, nh, rows),
        out_shape=(
            jax.ShapeDtypeStruct(attn_queries.shape, BF16),
            jax.ShapeDtypeStruct(attn_keys.shape, BF16),
            jax.ShapeDtypeStruct(attn_keys.shape, BF16),
        ),
        in_specs=[vmem] * 4,
        out_specs=(vmem,) * 3,
        scratch_shapes=[
            pltpu.VMEM((REACH + 1, nh) + block, BF16),
            pltpu.VMEM((nh, GROUP * rows, HD), BF16),
            pltpu.VMEM((nh, GROUP * rows, HD), BF16),
            pltpu.VMEM((3, nh) + block, F32),
            pltpu.VMEM((REACH, nh) + block, BF16),
            pltpu.VMEM((REACH, nh) + block, BF16),
            pltpu.VMEM((2 * REACH, rows, GROUP * rows), F32),
            pltpu.SemaphoreType.DMA((REACH, nh)),
            pltpu.SemaphoreType.DMA((REACH, nh)),
            pltpu.SemaphoreType.DMA((REACH, nh)),
            pltpu.SemaphoreType.DMA((REACH, nh)),
        ],
        compiler_params=pltpu.CompilerParams(
            collective_id=0, has_side_effects=True, vmem_limit_bytes=48 * 1024 * 1024
        ),
    )(attn_queries, attn_keys, attn_values, out_grad)
    partial_term = dot_tn(normed_input, key_low)
    summed = lax.psum_scatter(partial_term, "ctx", scatter_dimension=0, tiled=True)
    return (query_grad, summed, value_low)


def solution(mesh):
    return jax.shard_map(
        functools.partial(shards, mesh.shape["ctx"]),
        mesh=mesh,
        in_specs=(
            P(("groups", "ctx"), None),
            P(("groups", "ctx"), "tp"),
            P(("groups", "ctx"), "tp"),
            P(("groups", "ctx"), "tp"),
            P(("groups", "ctx"), "tp"),
        ),
        out_specs=(
            P(("groups", "ctx"), "tp"),
            P(("groups", "ctx"), "tp"),
            P(("groups", "ctx"), "tp"),
        ),
        check_vma=False,
    )
```

```python
import functools

import jax
import jax.numpy as jnp
from jax import lax
from jax.experimental import pallas as pl
from jax.experimental.pallas import tpu as pltpu
from jax.sharding import PartitionSpec as P

HD = 128
GROUP = 2
W = 1024
REACH = 4

attn_scale = 168.0 ** (-0.5)
LOG2E = 1.4426950408889634
NEG = -1e30
MESH = pl.DeviceIdType.MESH
F32 = jnp.float32
BF16 = jnp.bfloat16


def dot_nt(a, b):
    return lax.dot_general(a, b, (((1,), (1,)), ((), ())), preferred_element_type=F32)


def dot_nn(a, b):
    return lax.dot_general(a, b, (((1,), (0,)), ((), ())), preferred_element_type=F32)


def dot_tn(a, b):
    return lax.dot_general(a, b, (((0,), (0,)), ((), ())), preferred_element_type=F32)


def attention(
    n,
    nh,
    rows,
    fused,
    q_ref,
    k_ref,
    v_ref,
    g_ref,
    x_ref,
    dq_ref,
    dk_ref,
    dv_ref,
    buf,
    qp,
    gp,
    acc,
    sb,
    rv,
    s_sc,
    send_f,
    recv_f,
    send_r,
    recv_r,
    *more,
):
    c = lax.axis_index("ctx")
    x = lax.rem(c, 2)
    even = x == 0
    odd = x == 1
    pair = c + 1 - 2 * x
    up = c + 2 < n
    down = c >= 2

    barrier = pltpu.get_barrier_semaphore()

    def greet(target):
        pl.semaphore_signal(barrier, inc=1, device_id={"ctx": target}, device_id_type=MESH)

    if fused:
        x_half, x_turned, x_got, x_all, gath, x_sem = more[:6]
        send_x, recv_x, send_s, recv_s, send_p, recv_p, send_u, recv_u, send_d, recv_d = more[6:]
        core = lax.axis_index("tp")
        half = rows // 2
        out_rows = x_all.shape[0]
        load_x = pltpu.make_async_copy(
            x_ref.at[pl.ds(pl.multiple_of(core * half, half), half)], x_half, x_sem
        )
        load_x.start()
        for step in range(1, n):
            greet(lax.rem(c + step, n))
        pl.semaphore_signal(barrier, inc=1, device_id={"tp": 1 - core}, device_id_type=MESH)
    else:
        greet(pair)
        pl.when(up)(lambda: greet(c + 2))
        pl.when(down)(lambda: greet(c - 2))

    def cols(h, width):
        return pl.ds(pl.multiple_of(h * width, width), width)

    def pack(h, carry):
        buf[0, h, 0] = k_ref[:, cols(h, HD)]
        buf[0, h, 1] = v_ref[:, cols(h, HD)]
        return carry

    lax.fori_loop(0, nh, pack, 0)

    if fused:
        pl.semaphore_wait(barrier, n)
    else:
        pl.semaphore_wait(barrier, 1 + up.astype(jnp.int32) + down.astype(jnp.int32))

    def halo(src, dst, h, target):
        return pltpu.make_async_remote_copy(
            src_ref=buf.at[src, h],
            dst_ref=buf.at[dst, h],
            send_sem=send_f.at[dst - 1, h],
            recv_sem=recv_f.at[dst - 1, h],
            device_id={"ctx": target},
            device_id_type=MESH,
        )

    def back(d, h, target):
        return pltpu.make_async_remote_copy(
            src_ref=sb.at[d - 1, h],
            dst_ref=rv.at[d - 1, h],
            send_sem=send_r.at[d - 1, h],
            recv_sem=recv_r.at[d - 1, h],
            device_id={"ctx": target},
            device_id_type=MESH,
        )

    def send_own(h):
        pl.when(up)(lambda: halo(0, 2, h, c + 2).start())
        pl.when(even)(lambda: halo(0, 1, h, c + 1).start())

    send_own(0)
    send_own(1)

    def pack_q(h, carry):
        for i in range(GROUP):
            qp[h, i * rows : (i + 1) * rows] = q_ref[:, cols(h * GROUP + i, HD)]
            gp[h, i * rows : (i + 1) * rows] = g_ref[:, cols(h * GROUP + i, HD)]
        return carry

    lax.fori_loop(0, nh, pack_q, 0)

    if fused:
        z = c // 2
        nz = n // 2

        def x_copy(src, target):
            return pltpu.make_async_remote_copy(
                src_ref=x_turned.at[pl.ds(pl.multiple_of(target * out_rows, 16), out_rows)],
                dst_ref=x_got.at[src, core],
                send_sem=send_x.at[target],
                recv_sem=recv_x.at[src],
                device_id={"ctx": target},
                device_id_type=MESH,
            )

        def x_share(src, side):
            return pltpu.make_async_remote_copy(
                src_ref=x_got.at[src, side],
                dst_ref=x_got.at[src, side],
                send_sem=send_s.at[src],
                recv_sem=recv_s.at[src],
                device_id={"tp": 1 - core},
                device_id_type=MESH,
            )

        def gather_pair(h, block):
            return pltpu.make_async_remote_copy(
                src_ref=gath.at[h, block],
                dst_ref=gath.at[h, block],
                send_sem=send_p.at[h],
                recv_sem=recv_p.at[h],
                device_id={"ctx": pair},
                device_id_type=MESH,
            )

        def gather_line(h, level, target, send, recv):
            blocks = gath.at[h, pl.ds(level * 2, 2)]
            return pltpu.make_async_remote_copy(
                src_ref=blocks,
                dst_ref=blocks,
                send_sem=send.at[level, h],
                recv_sem=recv.at[level, h],
                device_id={"ctx": target},
                device_id_type=MESH,
            )

        def gather_up(h, level, target):
            return gather_line(h, level, target, send_u, recv_u)

        def gather_down(h, level, target):
            return gather_line(h, level, target, send_d, recv_d)

        load_x.wait()
        for at in range(0, x_half.shape[1], HD):
            x_turned[at : at + HD] = x_half[:, at : at + HD].T

        def send_x_if(wanted):
            def one(target, carry):
                @pl.when(wanted(target))
                def _():
                    x_copy(c, target).start()

                return carry

            lax.fori_loop(0, n, one, 0)

        send_x_if(lambda target: target < c)
        x_got[c, core] = x_turned[pl.ds(pl.multiple_of(c * out_rows, 16), out_rows)]
        x_share(c, core).start()

        def share_x(src, carry):
            @pl.when(src != c)
            def _():
                x_copy(src, lax.rem(c + 1, n)).wait_recv()
                x_share(src, core).start()

            return carry

        def collect_x():
            for src in range(n):
                x_share(src, 1 - core).wait_recv()
            for src in range(n):
                for side in range(2):
                    at = src * rows + side * half
                    x_all[:, at : at + half] = x_got[src, side]

        def gather_first(h):
            gather_pair(h, pair).wait_recv()
            pl.when(up)(lambda: gather_up(h, z, c + 2).start())
            pl.when(down)(lambda: gather_down(h, z, c - 2).start())

        def gather_hop(k, h):
            @pl.when(z >= k)
            def _():
                gather_up(h, z - k, pair).wait_recv()
                pl.when(up)(lambda: gather_up(h, z - k, c + 2).start())

            @pl.when(z + k < nz)
            def _():
                gather_down(h, z + k, pair).wait_recv()
                pl.when(down)(lambda: gather_down(h, z + k, c - 2).start())

        def project(h):
            dk_ref[:, cols(h, HD)] = dot_nn(x_all[...], gath[h].reshape(n * rows, HD))

    for d in range(1, REACH + 1):

        @pl.when(c < d)
        def _():
            buf[d] = jnp.zeros(buf.shape[1:], BF16)

    def forward(h):
        @pl.when(down)
        def _():
            halo(0, 2, h, pair).wait_recv()

            @pl.when(up)
            def _():
                halo(2, 4, h, c + 2).start()

            @pl.when(even)
            def _():
                halo(2, 3, h, pair).start()

            @pl.when(odd)
            def _():
                halo(2, 1, h, pair).start()

        @pl.when(h + 2 < nh)
        def _():
            send_own(h + 2)

        @pl.when(c >= 4)
        def _():
            halo(2, 4, h, pair).wait_recv()

            @pl.when(odd)
            def _():
                halo(4, 3, h, pair).start()

        pl.when(c >= 1)(lambda: halo(0, 1, h, pair).wait_recv())
        pl.when(c >= 3)(lambda: halo(0, 3, h, pair).wait_recv())

    wide = GROUP * rows
    key_at = lax.broadcasted_iota(jnp.int32, (rows, wide), 0)
    query_at = lax.rem(lax.broadcasted_iota(jnp.int32, (rows, wide), 1), rows)

    def compute(h):
        q = qp[h]
        g = gp[h]
        tri = key_at <= query_at
        factor = attn_scale * LOG2E
        far = jnp.where(c >= 4, 0.0, NEG)
        s0 = jnp.where(tri, dot_nt(buf[0, h, 0], q) * factor, dot_nt(buf[4, h, 0], q) * factor + far)
        s_sc[0] = s0
        top = jnp.max(s0, axis=0, keepdims=True)
        for d in range(1, REACH):
            s = dot_nt(buf[d, h, 0], q) * factor + jnp.where(c >= d, 0.0, NEG)
            s_sc[d] = s
            top = jnp.maximum(top, jnp.max(s, axis=0, keepdims=True))
        total = jnp.zeros((1, wide), F32)
        delta = jnp.zeros((1, wide), F32)
        for d in range(REACH):
            e = jnp.exp2(s_sc[d] - top)
            if d == 0:
                gpr = jnp.where(tri, dot_nt(buf[0, h, 1], g), dot_nt(buf[4, h, 1], g))
            else:
                gpr = dot_nt(buf[d, h, 1], g)
            total += jnp.sum(e, axis=0, keepdims=True)
            delta += jnp.sum(e * gpr, axis=0, keepdims=True)
            s_sc[d] = e
            s_sc[REACH + d] = gpr
        inv = 1.0 / total
        delta = delta * inv
        dq = jnp.zeros((HD, wide), F32)
        for d in range(REACH):
            p = s_sc[d] * inv
            ds = p * (s_sc[REACH + d] - delta)
            if d == 0:
                parts = (
                    (0, jnp.where(tri, p, 0.0), jnp.where(tri, ds, 0.0)),
                    (4, jnp.where(tri, 0.0, p), jnp.where(tri, 0.0, ds)),
                )
            else:
                parts = ((d, p, ds),)
            for slot, p_part, ds_part in parts:
                p_low = p_part.astype(BF16)
                ds_low = ds_part.astype(BF16)
                dk = attn_scale * dot_nn(ds_low, q)
                dv = dot_nn(p_low, g)
                dq += dot_tn(buf[slot, h, 0], ds_low)
                if slot % 2:
                    sb[slot - 1, h, 0] = dk.astype(BF16)
                    sb[slot - 1, h, 1] = dv.astype(BF16)
                else:
                    acc[slot // 2, h, 0] = dk
                    acc[slot // 2, h, 1] = dv
        dq = (dq * attn_scale).T.astype(BF16)
        for i in range(GROUP):
            dq_ref[:, cols(h * GROUP + i, HD)] = dq[i * rows : (i + 1) * rows]

        pl.when(c >= 1)(lambda: back(1, h, pair).start())
        pl.when(c >= 3)(lambda: back(3, h, pair).start())

    def add(slot, d, h):
        acc[slot, h] += rv[d - 1, h].astype(F32)

    def stage_b(h):
        @pl.when(pair >= 3)
        def _():
            back(3, h, pair).wait_recv()
            pl.when(odd)(lambda: add(2, 3, h))
            pl.when(even)(lambda: add(1, 3, h))

        @pl.when(c >= 4)
        def _():
            sb[3, h] = acc[2, h].astype(BF16)
            back(4, h, c - 2).start()

        @pl.when(pair >= 1)
        def _():
            back(1, h, pair).wait_recv()
            pl.when(odd)(lambda: add(1, 1, h))
            pl.when(even)(lambda: add(0, 1, h))

    def stage_c(h):
        @pl.when(down)
        def _():
            @pl.when(up)
            def _():
                back(4, h, pair).wait_recv()
                add(1, 4, h)

            sb[1, h] = acc[1, h].astype(BF16)
            back(2, h, c - 2).start()

    def stage_d(h):
        @pl.when(up)
        def _():
            back(2, h, pair).wait_recv()
            add(0, 2, h)

        if fused:
            gath[h, c] = acc[0, h, 0].astype(BF16)
            gather_pair(h, c).start()
        else:
            dk_ref[:, cols(h, HD)] = acc[0, h, 0].astype(BF16)
        dv_ref[:, cols(h, HD)] = acc[0, h, 1].astype(BF16)

    def step(i, carry):
        @pl.when(i < nh)
        def _():
            forward(i)
            if fused:
                pl.when(i == min(2, nh - 1))(lambda: send_x_if(lambda target: target > c))
            compute(i)

        @pl.when((i >= 1) & (i < nh + 1))
        def _():
            stage_b(i - 1)

        @pl.when((i >= 2) & (i < nh + 2))
        def _():
            stage_c(i - 2)

        @pl.when((i >= 3) & (i < nh + 3))
        def _():
            stage_d(i - 3)

        if fused:

            @pl.when((i >= 4) & (i < nh + 4))
            def _():
                gather_first(i - 4)

            for k in range(1, nz):

                @pl.when((i >= 4 + k) & (i < nh + 4 + k))
                def _():
                    gather_hop(k, i - 4 - k)

            @pl.when(i == nh + 1)
            def _():
                lax.fori_loop(0, n, share_x, 0)

            pl.when(i == nh + 3)(collect_x)

            @pl.when(i >= last)
            def _():
                project(i - last)

        return carry

    last = max(3 + n // 2, nh + 3) if fused else 3
    lax.fori_loop(0, nh + last, step, 0)

    def drain(h, carry):
        pl.when(up)(lambda: halo(0, 2, h, pair).wait_send())
        pl.when(even)(lambda: halo(0, 1, h, pair).wait_send())
        pl.when(down & up)(lambda: halo(2, 4, h, pair).wait_send())
        pl.when(down & even)(lambda: halo(2, 3, h, pair).wait_send())
        pl.when(down & odd)(lambda: halo(2, 1, h, pair).wait_send())
        pl.when((c >= 4) & odd)(lambda: halo(4, 3, h, pair).wait_send())
        pl.when(c >= 1)(lambda: back(1, h, pair).wait_send())
        pl.when(c >= 3)(lambda: back(3, h, pair).wait_send())
        pl.when(c >= 4)(lambda: back(4, h, pair).wait_send())
        pl.when(down)(lambda: back(2, h, pair).wait_send())
        if fused:
            gather_pair(h, c).wait_send()
            for level in range(nz):
                pl.when(up & (level <= z))(lambda: gather_up(h, level, pair).wait_send())
                pl.when(down & (level >= z))(lambda: gather_down(h, level, pair).wait_send())
        return carry

    lax.fori_loop(0, nh, drain, 0)
    if fused:

        def drain_x(src, carry):
            pl.when(src != c)(lambda: x_copy(c, src).wait_send())
            x_share(src, core).wait_send()
            return carry

        lax.fori_loop(0, n, drain_x, 0)


def shards(n, normed_input, attn_queries, attn_keys, attn_values, out_grad):
    rows = attn_queries.shape[0]
    nh = attn_keys.shape[1] // HD
    width = normed_input.shape[1]
    assert rows * REACH == W and n % 2 == 0
    fused = n <= 16 and width % n == 0 and (width // n) % 16 == 0 and width % HD == 0
    block = (2, rows, HD)
    vmem = pl.BlockSpec(memory_space=pltpu.VMEM)
    dma = pltpu.SemaphoreType.DMA
    scratch = [
        pltpu.VMEM((REACH + 1, nh) + block, BF16),
        pltpu.VMEM((nh, GROUP * rows, HD), BF16),
        pltpu.VMEM((nh, GROUP * rows, HD), BF16),
        pltpu.VMEM((3, nh) + block, F32),
        pltpu.VMEM((REACH, nh) + block, BF16),
        pltpu.VMEM((REACH, nh) + block, BF16),
        pltpu.VMEM((2 * REACH, rows, GROUP * rows), F32),
    ] + [dma((REACH, nh))] * 4
    if fused:
        key_out = jax.ShapeDtypeStruct((width // n, attn_keys.shape[1]), F32)
        scratch += [
            pltpu.VMEM((rows // 2, width), BF16),
            pltpu.VMEM((width, rows // 2), BF16),
            pltpu.VMEM((n, 2, width // n, rows // 2), BF16),
            pltpu.VMEM((width // n, n * rows), BF16),
            pltpu.VMEM((nh, n, rows, HD), BF16),
            dma,
        ]
        scratch += [dma((n,))] * 4 + [dma((nh,))] * 2 + [dma((n // 2, nh))] * 4
    else:
        key_out = jax.ShapeDtypeStruct(attn_keys.shape, BF16)
    query_grad, key_result, value_low = pl.pallas_call(
        functools.partial(attention, n, nh, rows, fused),
        out_shape=(
            jax.ShapeDtypeStruct(attn_queries.shape, BF16),
            key_out,
            jax.ShapeDtypeStruct(attn_keys.shape, BF16),
        ),
        in_specs=[vmem] * 4 + [pl.BlockSpec(memory_space=pl.ANY)],
        out_specs=(vmem,) * 3,
        scratch_shapes=scratch,
        compiler_params=pltpu.CompilerParams(
            collective_id=0, has_side_effects=True, vmem_limit_bytes=48 * 1024 * 1024
        ),
    )(attn_queries, attn_keys, attn_values, out_grad, normed_input)
    if not fused:
        partial_term = dot_tn(normed_input, key_result)
        key_result = lax.psum_scatter(partial_term, "ctx", scatter_dimension=0, tiled=True)
    return (query_grad, key_result, value_low)


def solution(mesh):
    return jax.shard_map(
        functools.partial(shards, mesh.shape["ctx"]),
        mesh=mesh,
        in_specs=(
            P(("groups", "ctx"), None),
            P(("groups", "ctx"), "tp"),
            P(("groups", "ctx"), "tp"),
            P(("groups", "ctx"), "tp"),
            P(("groups", "ctx"), "tp"),
        ),
        out_specs=(
            P(("groups", "ctx"), "tp"),
            P(("groups", "ctx"), "tp"),
            P(("groups", "ctx"), "tp"),
        ),
        check_vma=False,
    )
```

```python
import functools

import jax
import jax.numpy as jnp
from jax import lax
from jax.experimental import pallas as pl
from jax.experimental.pallas import tpu as pltpu
from jax.sharding import PartitionSpec as P

HD = 128
GROUP = 2
W = 1024
REACH = 4

attn_scale = 168.0 ** (-0.5)
LOG2E = 1.4426950408889634
NEG = -1e30
MESH = pl.DeviceIdType.MESH
F32 = jnp.float32
BF16 = jnp.bfloat16


def dot_nt(a, b):
    return lax.dot_general(a, b, (((1,), (1,)), ((), ())), preferred_element_type=F32)


def dot_nn(a, b):
    return lax.dot_general(a, b, (((1,), (0,)), ((), ())), preferred_element_type=F32)


def dot_tn(a, b):
    return lax.dot_general(a, b, (((0,), (0,)), ((), ())), preferred_element_type=F32)


def attention(
    n,
    nh,
    rows,
    fused,
    q_ref,
    k_ref,
    v_ref,
    g_ref,
    x_ref,
    dq_ref,
    dk_ref,
    dv_ref,
    buf,
    qp,
    gp,
    acc,
    sb,
    rv,
    s_sc,
    send_f,
    recv_f,
    send_r,
    recv_r,
    *more,
):
    c = lax.axis_index("ctx")
    x = lax.rem(c, 2)
    even = x == 0
    odd = x == 1
    pair = c + 1 - 2 * x
    up = c + 2 < n
    down = c >= 2

    barrier = pltpu.get_barrier_semaphore()

    def greet(target):
        pl.semaphore_signal(barrier, inc=1, device_id={"ctx": target}, device_id_type=MESH)

    if fused:
        x_half, x_turned, x_got, x_all, gath, give, take, x_sem = more[:8]
        send_x, recv_x, send_s, recv_s, send_p, recv_p, send_u, recv_u, send_d, recv_d = more[8:]
        core = lax.axis_index("tp")
        half = rows // 2
        out_rows = x_all.shape[0]
        own_rows = out_rows // 2
        load_x = pltpu.make_async_copy(
            x_ref.at[pl.ds(pl.multiple_of(core * half, half), half)], x_half, x_sem
        )
        load_x.start()
        for step in range(1, n):
            greet(lax.rem(c + step, n))
        pl.semaphore_signal(barrier, inc=1, device_id={"tp": 1 - core}, device_id_type=MESH)
    else:
        greet(pair)
        pl.when(up)(lambda: greet(c + 2))
        pl.when(down)(lambda: greet(c - 2))

    def cols(h, width):
        return pl.ds(pl.multiple_of(h * width, width), width)

    def pack(h, carry):
        buf[0, h, 0] = k_ref[:, cols(h, HD)]
        buf[0, h, 1] = v_ref[:, cols(h, HD)]
        return carry

    lax.fori_loop(0, nh, pack, 0)

    if fused:
        pl.semaphore_wait(barrier, n)
    else:
        pl.semaphore_wait(barrier, 1 + up.astype(jnp.int32) + down.astype(jnp.int32))

    def halo(src, dst, h, target):
        return pltpu.make_async_remote_copy(
            src_ref=buf.at[src, h],
            dst_ref=buf.at[dst, h],
            send_sem=send_f.at[dst - 1, h],
            recv_sem=recv_f.at[dst - 1, h],
            device_id={"ctx": target},
            device_id_type=MESH,
        )

    def back(d, h, target):
        return pltpu.make_async_remote_copy(
            src_ref=sb.at[d - 1, h],
            dst_ref=rv.at[d - 1, h],
            send_sem=send_r.at[d - 1, h],
            recv_sem=recv_r.at[d - 1, h],
            device_id={"ctx": target},
            device_id_type=MESH,
        )

    def send_own(h):
        pl.when(up)(lambda: halo(0, 2, h, c + 2).start())
        pl.when(even)(lambda: halo(0, 1, h, c + 1).start())

    send_own(0)
    send_own(1)

    def pack_q(h, carry):
        for i in range(GROUP):
            qp[h, i * rows : (i + 1) * rows] = q_ref[:, cols(h * GROUP + i, HD)]
            gp[h, i * rows : (i + 1) * rows] = g_ref[:, cols(h * GROUP + i, HD)]
        return carry

    lax.fori_loop(0, nh, pack_q, 0)

    if fused:
        z = c // 2
        nz = n // 2

        def x_copy(src, target):
            return pltpu.make_async_remote_copy(
                src_ref=x_turned.at[pl.ds(pl.multiple_of(target * out_rows, 16), out_rows)],
                dst_ref=x_got.at[src, core],
                send_sem=send_x.at[target],
                recv_sem=recv_x.at[src],
                device_id={"ctx": target * 2 + x},
                device_id_type=MESH,
            )

        def x_share(src, side):
            return pltpu.make_async_remote_copy(
                src_ref=x_got.at[src, side],
                dst_ref=x_got.at[src, side],
                send_sem=send_s.at[src],
                recv_sem=recv_s.at[src],
                device_id={"tp": 1 - core},
                device_id_type=MESH,
            )

        def trade(h):
            return pltpu.make_async_remote_copy(
                src_ref=give.at[h],
                dst_ref=take.at[h],
                send_sem=send_p.at[h],
                recv_sem=recv_p.at[h],
                device_id={"ctx": pair},
                device_id_type=MESH,
            )

        def gather_line(h, level, target, send, recv):
            blocks = gath.at[h, level]
            return pltpu.make_async_remote_copy(
                src_ref=blocks,
                dst_ref=blocks,
                send_sem=send.at[level, h],
                recv_sem=recv.at[level, h],
                device_id={"ctx": target},
                device_id_type=MESH,
            )

        def gather_up(h, level, target):
            return gather_line(h, level, target, send_u, recv_u)

        def gather_down(h, level, target):
            return gather_line(h, level, target, send_d, recv_d)

        load_x.wait()
        for at in range(0, x_half.shape[1], HD):
            x_turned[at : at + HD] = x_half[:, at : at + HD].T

        def send_x_if(wanted):
            def one(target, carry):
                @pl.when(wanted(target))
                def _():
                    x_copy(z, target).start()

                return carry

            lax.fori_loop(0, nz, one, 0)

        send_x_if(lambda target: target < z)
        x_got[z, core] = x_turned[pl.ds(pl.multiple_of(z * out_rows, 16), out_rows)]
        x_share(z, core).start()

        def share_x(src, carry):
            @pl.when(src != z)
            def _():
                x_copy(src, lax.rem(z + 1, nz)).wait_recv()
                x_share(src, core).start()

            return carry

        def collect_x():
            for src in range(nz):
                x_share(src, 1 - core).wait_recv()
            for src in range(nz):
                for side in range(2):
                    at = src * rows + side * half
                    x_all[:, at : at + half] = x_got[src, side]

        def gather_first(h):
            pl.when(up)(lambda: gather_up(h, z, c + 2).start())
            pl.when(down)(lambda: gather_down(h, z, c - 2).start())

        def gather_hop(k, h):
            @pl.when(z >= k)
            def _():
                gather_up(h, z - k, pair).wait_recv()
                pl.when(up)(lambda: gather_up(h, z - k, c + 2).start())

            @pl.when(z + k < nz)
            def _():
                gather_down(h, z + k, pair).wait_recv()
                pl.when(down)(lambda: gather_down(h, z + k, c - 2).start())

        def project(h):
            blocks = gath[h].reshape(nz * rows, HD)

            def part(side):
                return dot_nn(x_all[pl.ds(pl.multiple_of(side * own_rows, 16), own_rows)], blocks)

            give[h] = part(1 - x).astype(BF16)
            trade(h).start()
            dk_ref[:, cols(h, HD)] = part(x)

        def finish(h):
            trade(h).wait_recv()
            dk_ref[:, cols(h, HD)] += take[h].astype(F32)

    for d in range(1, REACH + 1):

        @pl.when(c < d)
        def _():
            buf[d] = jnp.zeros(buf.shape[1:], BF16)

    def forward(h):
        @pl.when(down)
        def _():
            halo(0, 2, h, pair).wait_recv()

            @pl.when(up)
            def _():
                halo(2, 4, h, c + 2).start()

            @pl.when(even)
            def _():
                halo(2, 3, h, pair).start()

            @pl.when(odd)
            def _():
                halo(2, 1, h, pair).start()

        @pl.when(h + 2 < nh)
        def _():
            send_own(h + 2)

    def forward_far(h):
        @pl.when(c >= 4)
        def _():
            halo(2, 4, h, pair).wait_recv()

            @pl.when(odd)
            def _():
                halo(4, 3, h, pair).start()

    def arrived(h):
        pl.when(c >= 1)(lambda: halo(0, 1, h, pair).wait_recv())
        pl.when(c >= 3)(lambda: halo(0, 3, h, pair).wait_recv())

    wide = GROUP * rows
    key_at = lax.broadcasted_iota(jnp.int32, (rows, wide), 0)
    query_at = lax.rem(lax.broadcasted_iota(jnp.int32, (rows, wide), 1), rows)

    def compute(h):
        q = qp[h]
        g = gp[h]
        tri = key_at <= query_at
        factor = attn_scale * LOG2E
        far = jnp.where(c >= 4, 0.0, NEG)
        s0 = jnp.where(tri, dot_nt(buf[0, h, 0], q) * factor, dot_nt(buf[4, h, 0], q) * factor + far)
        s_sc[0] = s0
        top = jnp.max(s0, axis=0, keepdims=True)
        for d in range(1, REACH):
            s = dot_nt(buf[d, h, 0], q) * factor + jnp.where(c >= d, 0.0, NEG)
            s_sc[d] = s
            top = jnp.maximum(top, jnp.max(s, axis=0, keepdims=True))
        total = jnp.zeros((1, wide), F32)
        delta = jnp.zeros((1, wide), F32)
        for d in range(REACH):
            e = jnp.exp2(s_sc[d] - top)
            if d == 0:
                gpr = jnp.where(tri, dot_nt(buf[0, h, 1], g), dot_nt(buf[4, h, 1], g))
            else:
                gpr = dot_nt(buf[d, h, 1], g)
            total += jnp.sum(e, axis=0, keepdims=True)
            delta += jnp.sum(e * gpr, axis=0, keepdims=True)
            s_sc[d] = e
            s_sc[REACH + d] = gpr
        inv = 1.0 / total
        delta = delta * inv
        dq = jnp.zeros((HD, wide), F32)
        for d in range(REACH):
            p = s_sc[d] * inv
            ds = p * (s_sc[REACH + d] - delta)
            if d == 0:
                parts = (
                    (0, jnp.where(tri, p, 0.0), jnp.where(tri, ds, 0.0)),
                    (4, jnp.where(tri, 0.0, p), jnp.where(tri, 0.0, ds)),
                )
            else:
                parts = ((d, p, ds),)
            for slot, p_part, ds_part in parts:
                p_low = p_part.astype(BF16)
                ds_low = ds_part.astype(BF16)
                dk = attn_scale * dot_nn(ds_low, q)
                dv = dot_nn(p_low, g)
                dq += dot_tn(buf[slot, h, 0], ds_low)
                if slot % 2:
                    sb[slot - 1, h, 0] = dk.astype(BF16)
                    sb[slot - 1, h, 1] = dv.astype(BF16)
                else:
                    acc[slot // 2, h, 0] = dk
                    acc[slot // 2, h, 1] = dv
        dq = (dq * attn_scale).T.astype(BF16)
        for i in range(GROUP):
            dq_ref[:, cols(h * GROUP + i, HD)] = dq[i * rows : (i + 1) * rows]

        pl.when(c >= 1)(lambda: back(1, h, pair).start())
        pl.when(c >= 3)(lambda: back(3, h, pair).start())

    def add(slot, d, h):
        acc[slot, h] += rv[d - 1, h].astype(F32)

    def stage_b(h):
        @pl.when(pair >= 3)
        def _():
            back(3, h, pair).wait_recv()
            pl.when(odd)(lambda: add(2, 3, h))
            pl.when(even)(lambda: add(1, 3, h))

        @pl.when(c >= 4)
        def _():
            sb[3, h] = acc[2, h].astype(BF16)
            back(4, h, c - 2).start()

        @pl.when(pair >= 1)
        def _():
            back(1, h, pair).wait_recv()
            pl.when(odd)(lambda: add(1, 1, h))
            pl.when(even)(lambda: add(0, 1, h))

    def stage_c(h):
        @pl.when(down)
        def _():
            @pl.when(up)
            def _():
                back(4, h, pair).wait_recv()
                add(1, 4, h)

            sb[1, h] = acc[1, h].astype(BF16)
            back(2, h, c - 2).start()

    def stage_d(h):
        @pl.when(up)
        def _():
            back(2, h, pair).wait_recv()
            add(0, 2, h)

        if fused:
            gath[h, z] = acc[0, h, 0].astype(BF16)
            gather_first(h)
        else:
            dk_ref[:, cols(h, HD)] = acc[0, h, 0].astype(BF16)
        dv_ref[:, cols(h, HD)] = acc[0, h, 1].astype(BF16)

    def stage(i, lag, run):
        pl.when((i >= lag) & (i < nh + lag))(lambda: run(i - lag))

    def step(i, carry):
        stage(i, 0, forward)
        stage(i, 1, forward_far)
        if fused:
            pl.when(i == nh)(lambda: send_x_if(lambda target: target > z))
        stage(i, 2, arrived)
        stage(i, 2, compute)
        stage(i, 3, stage_b)
        stage(i, 4, stage_c)
        stage(i, 5, stage_d)
        if fused:
            for k in range(1, nz):
                stage(i, 5 + k, functools.partial(gather_hop, k))

            @pl.when(i == nh + 4)
            def _():
                lax.fori_loop(0, nz, share_x, 0)

            pl.when(i == last)(collect_x)
            stage(i, last, project)
            stage(i, last + 1, finish)
        return carry

    last = max(4 + n // 2, nh + 5) if fused else 5
    lax.fori_loop(0, nh + last + (1 if fused else 0), step, 0)

    def drain(h, carry):
        pl.when(up)(lambda: halo(0, 2, h, pair).wait_send())
        pl.when(even)(lambda: halo(0, 1, h, pair).wait_send())
        pl.when(down & up)(lambda: halo(2, 4, h, pair).wait_send())
        pl.when(down & even)(lambda: halo(2, 3, h, pair).wait_send())
        pl.when(down & odd)(lambda: halo(2, 1, h, pair).wait_send())
        pl.when((c >= 4) & odd)(lambda: halo(4, 3, h, pair).wait_send())
        pl.when(c >= 1)(lambda: back(1, h, pair).wait_send())
        pl.when(c >= 3)(lambda: back(3, h, pair).wait_send())
        pl.when(c >= 4)(lambda: back(4, h, pair).wait_send())
        pl.when(down)(lambda: back(2, h, pair).wait_send())
        if fused:
            trade(h).wait_send()
            for level in range(nz):
                pl.when(up & (level <= z))(lambda: gather_up(h, level, pair).wait_send())
                pl.when(down & (level >= z))(lambda: gather_down(h, level, pair).wait_send())
        return carry

    lax.fori_loop(0, nh, drain, 0)
    if fused:

        def drain_x(src, carry):
            pl.when(src != z)(lambda: x_copy(z, src).wait_send())
            x_share(src, core).wait_send()
            return carry

        lax.fori_loop(0, nz, drain_x, 0)


def shards(n, normed_input, attn_queries, attn_keys, attn_values, out_grad):
    rows = attn_queries.shape[0]
    nh = attn_keys.shape[1] // HD
    width = normed_input.shape[1]
    assert rows * REACH == W and n % 2 == 0
    fused = n <= 16 and width % n == 0 and (width // n) % 16 == 0 and width % HD == 0
    block = (2, rows, HD)
    vmem = pl.BlockSpec(memory_space=pltpu.VMEM)
    dma = pltpu.SemaphoreType.DMA
    scratch = [
        pltpu.VMEM((REACH + 1, nh) + block, BF16),
        pltpu.VMEM((nh, GROUP * rows, HD), BF16),
        pltpu.VMEM((nh, GROUP * rows, HD), BF16),
        pltpu.VMEM((3, nh) + block, F32),
        pltpu.VMEM((REACH, nh) + block, BF16),
        pltpu.VMEM((REACH, nh) + block, BF16),
        pltpu.VMEM((2 * REACH, rows, GROUP * rows), F32),
    ] + [dma((REACH, nh))] * 4
    if fused:
        key_out = jax.ShapeDtypeStruct((width // n, attn_keys.shape[1]), F32)
        scratch += [
            pltpu.VMEM((rows // 2, width), BF16),
            pltpu.VMEM((width, rows // 2), BF16),
            pltpu.VMEM((n // 2, 2, 2 * width // n, rows // 2), BF16),
            pltpu.VMEM((2 * width // n, n // 2 * rows), BF16),
            pltpu.VMEM((nh, n // 2, rows, HD), BF16),
            pltpu.VMEM((nh, width // n, HD), BF16),
            pltpu.VMEM((nh, width // n, HD), BF16),
            dma,
        ]
        scratch += [dma((n // 2,))] * 4 + [dma((nh,))] * 2 + [dma((n // 2, nh))] * 4
    else:
        key_out = jax.ShapeDtypeStruct(attn_keys.shape, BF16)
    query_grad, key_result, value_low = pl.pallas_call(
        functools.partial(attention, n, nh, rows, fused),
        out_shape=(
            jax.ShapeDtypeStruct(attn_queries.shape, BF16),
            key_out,
            jax.ShapeDtypeStruct(attn_keys.shape, BF16),
        ),
        in_specs=[vmem] * 4 + [pl.BlockSpec(memory_space=pl.ANY)],
        out_specs=(vmem,) * 3,
        scratch_shapes=scratch,
        compiler_params=pltpu.CompilerParams(
            collective_id=0, has_side_effects=True, vmem_limit_bytes=48 * 1024 * 1024
        ),
    )(attn_queries, attn_keys, attn_values, out_grad, normed_input)
    if not fused:
        partial_term = dot_tn(normed_input, key_result)
        key_result = lax.psum_scatter(partial_term, "ctx", scatter_dimension=0, tiled=True)
    return (query_grad, key_result, value_low)


def solution(mesh):
    return jax.shard_map(
        functools.partial(shards, mesh.shape["ctx"]),
        mesh=mesh,
        in_specs=(
            P(("groups", "ctx"), None),
            P(("groups", "ctx"), "tp"),
            P(("groups", "ctx"), "tp"),
            P(("groups", "ctx"), "tp"),
            P(("groups", "ctx"), "tp"),
        ),
        out_specs=(
            P(("groups", "ctx"), "tp"),
            P(("groups", "ctx"), "tp"),
            P(("groups", "ctx"), "tp"),
        ),
        check_vma=False,
    )
```
